768 devices in a mesh: em: 12 (over z), blk: 4 (over x), rep: 16 (over y, core).
Axes of the slice: x: 4, y: 8, z: 12, core: 2. Of those that a mesh axis runs over, the one named last changes fastest.
Arguments:
- green: bfloat16 [768, 4, 8, 128, 256], P(('em', 'rep'), None, 'blk'), may hold values from -6 to 6
- occupation: float32 [4], replicated, may hold values from 0.2 to 4
- offsets: int32 [4], replicated, may hold values from 1 to 2, as said below
- qtable: int32 [4, 4], replicated, may hold values from 0 to 3
- coupling: bfloat16 [8, 3, 128, 128], P('blk'), may hold values from -0.5 to 0.5
- pattern: int32 [8, 3], P('blk'), may hold values 0 or 1
Outputs:
- sigma: bfloat16 [768, 4, 8, 128, 256], P(('em', 'rep'), None, 'blk')
The draws below stay inside these ranges and needn't reach their ends.
Inputs may be any that keep to these rules, and one draw needn't show every extreme that they name: `offsets`: every offset lies in 1 .. 2 and one equals 2.
All inputs are finite; a program needn't handle non-finite values. No bound on the sum of `pattern` on one device may be relied on, other than what follows from the above.
Results may differ from the reference program's by a relative error of at most 0.0057.
Values may be sent and summed in bfloat16 or wider, within the bound.
No kernel may reach another device: no remote copies, remote signals or barrier semaphores. Data moves between devices by JAX's collectives and lax.ppermute only.
A program may use at most 64 MiB of HBM per device.

```python
import math
import jax
import jax.numpy as jnp
from jax import lax

ORB = 128
NK = 4
NQ = 4
NS = 4
OFF_MAX = 2
NE = 768
TILES = 8


def draw_offsets(key, part):
    key = jax.random.fold_in(key, 7)
    first, second = jax.random.split(key)
    values = jax.random.randint(first, (NS,), 1, OFF_MAX + 1)
    place = jax.random.randint(second, (), 0, NS)
    return jnp.where(jnp.arange(NS) == place, OFF_MAX, values).astype(jnp.int32)


def set_ends(values, stream_key, least, largest):
    spot = [jax.random.randint(jax.random.fold_in(stream_key, axis), (), 0, length) for axis, length in enumerate(values.shape)]
    longest = values.shape.index(max(values.shape))
    next_to = spot[:longest] + [(spot[longest] + 1) % values.shape[longest]] + spot[longest + 1:]
    return values.at[tuple(spot)].set(least).at[tuple(next_to)].set(largest)


def block_levels(stream_key, extent, cuts, smallest, largest):
    loudness, own = 1.0, jax.random.fold_in(stream_key, 6)
    for dim, shards_of in cuts:
        draws = jnp.exp(jax.random.uniform(jax.random.fold_in(own, dim), (shards_of,), jnp.float32, smallest / len(cuts), largest / len(cuts)))
        loudness = loudness * jnp.repeat(draws, extent[dim] // shards_of).reshape([-1 if axis == dim else 1 for axis in range(len(extent))])
    return loudness


def scatter_about(key, extent, deviation, limit, pieces=(), kind=jnp.bfloat16):
    factor_of = block_levels(key, extent, pieces, -0.22, 0.18) if pieces else 1.0
    array = jax.random.normal(key, extent, jnp.float32) * deviation * factor_of
    return jnp.minimum(jnp.maximum(array, -limit), limit).astype(kind)


def setup_inputs(seed: int = 0) -> dict:
    splits = jax.random.split(jax.random.key(seed), 7)
    return {
        "green": scatter_about(splits[0], (NE, NK, TILES, ORB, 2 * ORB), 1.0, 6.0, ((0, 192), (2, 4))),
        "occupation": jnp.clip(jnp.exp(jax.random.uniform(splits[1], (NS,), jnp.float32, math.log(0.2), math.log(4.0))), 0.2, 4.0),
        "offsets": draw_offsets(jax.random.fold_in(splits[6], 71), 0),
        "qtable": set_ends(jax.random.randint(splits[3], (NK, NQ), 0, NK), jax.random.fold_in(splits[3], 1), 0, NK - 1).astype(jnp.int32),
        "coupling": scatter_about(splits[4], (TILES, 3, ORB, ORB), ORB ** -0.5, 0.5, ((0, 4),)),
        "pattern": set_ends((jax.random.randint(splits[5], (TILES, 3), 0, 3) < 2).astype(jnp.int32), jax.random.fold_in(splits[5], 1), 0, 1),
    }


def reference(green, occupation, offsets, qtable, coupling, pattern):
    shifts = jnp.arange(2 * OFF_MAX + 1, dtype=jnp.int32) - OFF_MAX
    hits_up = (offsets[:, None] == shifts[None, :]).astype(jnp.float32)
    hits_down = (offsets[:, None] == -shifts[None, :]).astype(jnp.float32)
    band = jnp.sum((occupation[:, None] + 1.0) * hits_up + occupation[:, None] * hits_down, axis=0)
    momenta = jnp.arange(NK, dtype=jnp.int32)
    transfer = jnp.sum((qtable[:, :, None] == momenta[None, None, :]).astype(jnp.float32), axis=1) / NQ
    kern = (band[:, None, None] * transfer[None, :, :]).astype(jnp.bfloat16).astype(jnp.float32)
    padded = jnp.pad(green, ((OFF_MAX, OFF_MAX), (0, 0), (0, 0), (0, 0), (0, 0)))

    def aggregate(tile):
        block = lax.dynamic_index_in_dim(padded, tile, 2, keepdims=False)
        total = jnp.zeros((NE, NK, ORB, 2 * ORB), jnp.float32)
        for step in range(2 * OFF_MAX + 1):
            window = block[step:step + NE].astype(jnp.float32)
            total = total + jnp.einsum('kl,elrc->ekrc', kern[step], window, precision=lax.Precision.HIGHEST)
        return total.astype(jnp.bfloat16)

    agg = lax.map(aggregate, jnp.arange(TILES, dtype=jnp.int32))
    agg_pad = jnp.pad(agg, ((1, 1), (0, 0), (0, 0), (0, 0), (0, 0)))
    masked = coupling * pattern[:, :, None, None].astype(jnp.bfloat16)
    whole = masked.astype(jnp.float32)

    def tile_sigma(tile):
        total = jnp.zeros((NE, NK, ORB, 2, ORB), jnp.float32)
        blocks = lax.dynamic_index_in_dim(whole, tile, 0, keepdims=False)
        for near in range(3):
            nearby = lax.dynamic_index_in_dim(agg_pad, tile + near, 0, keepdims=False).astype(jnp.float32)
            matrix = blocks[near]
            left = jnp.einsum('dr,ekrc->ekdc', matrix, nearby, precision=lax.Precision.HIGHEST)
            left = left.reshape(NE, NK, ORB, 2, ORB)
            total = total + jnp.einsum('ekdpc,fc->ekdpf', left, matrix, precision=lax.Precision.HIGHEST)
        return total.reshape(NE, NK, ORB, 2 * ORB).astype(jnp.bfloat16)

    sigma = lax.map(tile_sigma, jnp.arange(TILES, dtype=jnp.int32))
    return jnp.transpose(sigma, (1, 2, 0, 3, 4))
```

```python
import jax
import jax.numpy as jnp
from jax import lax
from jax.experimental import pallas as pl
from jax.experimental.pallas import tpu as pltpu
from jax.sharding import PartitionSpec as P

REACH = 2
FIRST = 64
VMEM = pl.BlockSpec(memory_space=pltpu.VMEM)
SMEM = pl.BlockSpec(memory_space=pltpu.SMEM)
ANY = pl.BlockSpec(memory_space=pl.ANY)
PARAMS = pltpu.CompilerParams(vmem_limit_bytes=40 * 2**20)
BF16 = jnp.bfloat16


def swap_pairs(count, first):
    pairs = [(i, i + 1) for i in range(first, count - 1, 2)]
    return pairs + [(b, a) for a, b in pairs]


def edge_kernel(s_ref, green, first2, whole1, second2):
    rows = first2.shape[3]
    one, two = 2 - 2 * s_ref[2], 2 * s_ref[2]
    for e in range(REACH):
        first2[e] = green[two + e, :, :, :rows]
        whole1[e] = green[one + e]
        second2[e] = green[two + e, :, :, rows:]


def weight_kernel(s_ref, occupation, offsets, qtable, out):
    def band(d):
        total = 0.0
        for s in range(4):
            value = occupation[s] + 1.0 if d > 0 else occupation[s]
            total = total + jnp.where(offsets[s] == abs(d), value, 0.0)
        return total

    bands = {d: band(d) for d in (-2, -1, 1, 2)}
    lane = lax.broadcasted_iota(jnp.int32, (16, 128), 1)
    unit = lax.broadcasted_iota(jnp.int32, (16, 128), 0) == lane % 16
    transfer = []
    for k in range(4):
        row = jnp.zeros((16, 128), jnp.float32)
        for l in range(4):
            hits = sum(jnp.where(qtable[k, q] == l, 0.25, 0.0) for q in range(4))
            row = jnp.where(unit & ((lane // 16) % 4 == l), hits, row)
        transfer.append(row)

    def weight(even, odd):
        low, high = bands.get(even, 0.0), bands.get(odd, 0.0)
        return jnp.where(s_ref[2] == 1, high, low)

    for place, (even, odd) in enumerate(((4, -2), (0, 0), (2, 2), (-2, 4))):
        for e in range(4):
            left = weight(even - e, odd - e)
            right = weight(even - e + 1, odd - e + 1)
            scale = jnp.where(lane < 64, left, right)
            for k in range(4):
                at = pl.ds(64 * e + 16 * k, 16)
                out[at, place * 128 : (place + 1) * 128] = (scale * transfer[k]).astype(BF16)


def aggregate_rows(weights, side1, own, side2, out, out_row):
    blocks = [side1(e, l) for e in range(2) for l in range(4)]
    blocks += [own(e, l) for e in range(4) for l in range(4)]
    blocks += [side2(e, l) for e in range(2) for l in range(4)]
    total = jnp.dot(
        weights[...], jnp.concatenate(blocks, axis=0), preferred_element_type=jnp.float32
    ).astype(BF16)
    for e in range(4):
        for k in range(4):
            n = 16 * (4 * e + k)
            out[e, k, pl.ds(out_row, 16)] = total[n : n + 16]


def own_kernel(row, s_ref, weights, green, side1, side2, out1, out2):
    for slot, out in ((0, out1), (1, out2)):
        tile = s_ref[slot]

        def step(n, carry):
            r = pl.multiple_of(n * 16, 16)
            aggregate_rows(
                weights,
                lambda e, l: side1[e, l, tile, pl.ds(r + row, 16)],
                lambda e, l: green[e, l, tile, pl.ds(r + row, 16)],
                lambda e, l: side2[e, l, tile, pl.ds(r, 16)],
                out,
                r,
            )
            return carry

        lax.fori_loop(0, out.shape[2] // 16, step, 0, unroll=4)


TRANSPOSED = (((1,), (1,)), ((), ()))


def right_products(part, weight, p):
    rows = part.shape[2]
    lhs = part[:, :, :, p * 128 : (p + 1) * 128].reshape(16 * rows, 128)
    u = lax.dot_general(lhs, weight, TRANSPOSED, preferred_element_type=jnp.float32)
    return u.astype(BF16).reshape(16, rows, weight.shape[0])


def inner_kernel(s_ref, eff, first1, second1, first2, second2, out, work):
    tau = [s_ref[0], s_ref[1]]
    pair = [
        jnp.concatenate([eff[tau[0], 1], eff[tau[1], 2 - 2 * tau[1]]], axis=0),
        jnp.concatenate([eff[tau[0], 2 - 2 * tau[0]], eff[tau[1], 1]], axis=0),
    ]
    raw = first1.shape[2]
    for source, parts in enumerate(((first1, second1), (first2, second2))):
        for part, row in zip(parts, (0, raw)):
            for p in range(2):
                u = right_products(part, pair[source], p)
                at = pl.ds(source * 128 + row, part.shape[2])
                for a in range(2):
                    work[a, :, at, p * 128 : (p + 1) * 128] = u[:, :, a * 128 : (a + 1) * 128]
    stack = [
        jnp.concatenate([eff[tau[0], 1], eff[tau[0], 2 - 2 * tau[0]]], axis=1),
        jnp.concatenate([eff[tau[1], 2 - 2 * tau[1]], eff[tau[1], 1]], axis=1),
    ]

    def step(e, carry):
        for k in range(4):
            for a in range(2):
                out[e, k, a] = jnp.dot(
                    stack[a], work[a, 4 * e + k], preferred_element_type=jnp.float32
                )
        return carry

    lax.fori_loop(0, 4, step, 0, unroll=2)


def half_kernel(s_ref, eff, first1, first2, out):
    for a, part in enumerate((first1, first2)):
        rim = eff[s_ref[a], 2 * s_ref[a]]
        for p in range(2):
            out[a, :, :, p * 128 : (p + 1) * 128] = right_products(part, rim, p)


def final_kernel(s_ref, eff, inner, half, second1, second2, out, work, store, sems):
    tau = [s_ref[0], s_ref[1]]
    rim = [eff[tau[a], 2 * tau[a]] for a in range(2)]
    for a, part in enumerate((second1, second2)):
        for p in range(2):
            work[a, :, :, p * 128 : (p + 1) * 128] = right_products(part, rim[a], p)

    copies = []
    for e in range(4):
        for k in range(4):
            for a in range(2):
                right = jnp.concatenate([half[a, 4 * e + k], work[a, 4 * e + k]], axis=0)
                total = jnp.dot(rim[a], right, preferred_element_type=jnp.float32)
                store[e, k, tau[a]] = (inner[e, k, a] + total).astype(BF16)
        copies.append(pltpu.make_async_copy(store.at[e], out.at[e], sems.at[e]))
        copies[-1].start()
    for copy in copies:
        copy.wait()


def call(kernel, in_specs, shapes, args, name, out_specs=None, scratch=(), cost=1):
    out_specs = [VMEM] * len(shapes) if out_specs is None else out_specs
    return pl.pallas_call(
        kernel,
        in_specs=in_specs,
        out_specs=out_specs,
        out_shape=[jax.ShapeDtypeStruct(shape, dtype) for shape, dtype in shapes],
        scratch_shapes=list(scratch),
        compiler_params=PARAMS,
        cost_estimate=pl.CostEstimate(flops=cost, bytes_accessed=1, transcendentals=0),
        name=name,
    )(*args)


def local(green, occupation, offsets, qtable, coupling, pattern):
    e_axes = ("em", "rep")
    x1, x2 = swap_pairs(lax.axis_size("blk"), 0), swap_pairs(lax.axis_size("blk"), 1)
    y_count = lax.axis_size(e_axes)
    y1, y2 = swap_pairs(y_count, 0), swap_pairs(y_count, 1)
    odd = lax.axis_index("rep") % 2
    tau1 = 1 - lax.axis_index("blk") % 2
    scalars = jnp.stack([tau1, 1 - tau1, odd]).astype(jnp.int32)
    second = green.shape[3] - FIRST
    dma = pltpu.SemaphoreType.DMA

    first2, whole1, second2 = call(
        edge_kernel,
        [SMEM, VMEM],
        [((2, 4, 2, rows, 256), BF16) for rows in (FIRST, FIRST + second, second)],
        (scalars, green),
        "edge",
    )
    first2 = lax.ppermute(first2, e_axes, y2)
    whole1 = lax.ppermute(whole1, e_axes, y1)
    second2 = lax.ppermute(second2, e_axes, y2)

    (weights,) = call(
        weight_kernel,
        [SMEM] * 4,
        [((256, 512), BF16)],
        (scalars, occupation, offsets, qtable),
        "weights",
    )
    eff = coupling * pattern[:, :, None, None].astype(BF16)

    def own(row, rows, side2, name):
        def kernel(*refs):
            own_kernel(row, *refs)

        return call(
            kernel,
            [SMEM] + [VMEM] * 4,
            [((4, 4, rows, 256), BF16)] * 2,
            (scalars, weights, green, whole1, side2),
            name,
        )

    own_first1, own_first2 = own(0, FIRST, first2, "own_first")
    rim_first2 = lax.ppermute(own_first2, "blk", x2)
    rim_first1 = lax.ppermute(own_first1, "blk", x1)
    own_second1, own_second2 = own(FIRST, second, second2, "own_second")
    rim_second2 = lax.ppermute(own_second2, "blk", x2)
    rim_second1 = lax.ppermute(own_second1, "blk", x1)
    (inner,) = call(
        inner_kernel,
        [SMEM] + [VMEM] * 5,
        [((4, 4, 2, 128, 256), jnp.float32)],
        (scalars, eff, own_first1, own_second1, own_first2, own_second2),
        "inner",
        scratch=[pltpu.VMEM((2, 16, 256, 256), BF16)],
    )
    (half,) = call(
        half_kernel,
        [SMEM] + [VMEM] * 3,
        [((2, 16, FIRST, 256), BF16)],
        (scalars, eff, rim_first1, rim_first2),
        "half",
    )
    (sigma,) = call(
        final_kernel,
        [SMEM] + [VMEM] * 5,
        [(green.shape, BF16)],
        (scalars, eff, inner, half, rim_second1, rim_second2),
        "final",
        out_specs=[ANY],
        scratch=[
            pltpu.VMEM((2, 16, second, 256), BF16),
            pltpu.VMEM(green.shape, BF16),
            dma((4,)),
        ],
    )
    return sigma


def solution(mesh):
    in_specs = (
        P(("em", "rep"), None, "blk", None, None),
        P(),
        P(),
        P(),
        P("blk", None, None, None),
        P("blk", None),
    )
    out_specs = P(("em", "rep"), None, "blk", None, None)
    return jax.shard_map(local, mesh=mesh, in_specs=in_specs, out_specs=out_specs, check_vma=False)
```

```python
import jax
import jax.numpy as jnp
from jax import lax
from jax.experimental import pallas as pl
from jax.experimental.pallas import tpu as pltpu
from jax.sharding import PartitionSpec as P

REACH = 2
RAW = 64
VMEM = pl.BlockSpec(memory_space=pltpu.VMEM)
SMEM = pl.BlockSpec(memory_space=pltpu.SMEM)
HBM = pl.BlockSpec(memory_space=pltpu.HBM)
ANY = pl.BlockSpec(memory_space=pl.ANY)
PARAMS = pltpu.CompilerParams(vmem_limit_bytes=40 * 2**20)
BF16 = jnp.bfloat16


def swap_pairs(count, first):
    pairs = [(i, i + 1) for i in range(first, count - 1, 2)]
    return pairs + [(b, a) for a, b in pairs]


def load_kernel(s_ref, green, raw2, raw1, late2, whole1, early2):
    raw = early2.shape[3]
    one, two = 2 - 2 * s_ref[2], 2 * s_ref[2]
    for e in range(4):
        raw2[e] = green[e, :, s_ref[1], :raw]
        raw1[e] = green[e, :, s_ref[0], :raw]
    for e in range(REACH):
        late2[e] = green[two + e, :, :, raw:]
        whole1[e] = green[one + e]
        early2[e] = green[two + e, :, :, :raw]


def far_kernel(s_ref, raw2, raw1, after, far2, far1):
    del after
    one, two = 2 - 2 * s_ref[2], 2 * s_ref[2]
    for slot, raw in enumerate((raw1, raw2)):
        for e in range(REACH):
            for l in range(4):
                far2[8 * e + 2 * l + slot] = raw[two + e, l]
                far1[8 * e + 2 * l + slot] = raw[one + e, l]
    far2[16] = jnp.zeros(far2.shape[1:], BF16)


def weight_kernel(s_ref, occupation, offsets, qtable, out):
    def band(d):
        total = 0.0
        for s in range(4):
            value = occupation[s] + 1.0 if d > 0 else occupation[s]
            total = total + jnp.where(offsets[s] == abs(d), value, 0.0)
        return total

    bands = {d: band(d) for d in (-2, -1, 1, 2)}
    lane = lax.broadcasted_iota(jnp.int32, (16, 128), 1)
    unit = lax.broadcasted_iota(jnp.int32, (16, 128), 0) == lane % 16
    transfer = []
    for k in range(4):
        row = jnp.zeros((16, 128), jnp.float32)
        for l in range(4):
            hits = sum(jnp.where(qtable[k, q] == l, 0.25, 0.0) for q in range(4))
            row = jnp.where(unit & ((lane // 16) % 4 == l), hits, row)
        transfer.append(row)

    def weight(even, odd):
        low, high = bands.get(even, 0.0), bands.get(odd, 0.0)
        return jnp.where(s_ref[2] == 1, high, low)

    for place, (even, odd) in enumerate(((4, -2), (0, 0), (2, 2), (-2, 4))):
        for e in range(4):
            left = weight(even - e, odd - e)
            right = weight(even - e + 1, odd - e + 1)
            scale = jnp.where(lane < 64, left, right)
            for k in range(4):
                at = pl.ds(64 * e + 16 * k, 16)
                out[at, place * 128 : (place + 1) * 128] = (scale * transfer[k]).astype(BF16)


def aggregate_rows(weights, side1, own, side2, out, out_row):
    blocks = [side1(e, l) for e in range(2) for l in range(4)]
    blocks += [own(e, l) for e in range(4) for l in range(4)]
    blocks += [side2(e, l) for e in range(2) for l in range(4)]
    total = jnp.dot(
        weights[...], jnp.concatenate(blocks, axis=0), preferred_element_type=jnp.float32
    ).astype(BF16)
    for e in range(4):
        for k in range(4):
            n = 16 * (4 * e + k)
            out[e, k, pl.ds(out_row, 16)] = total[n : n + 16]


def own_kernel(row, side1_row, s_ref, weights, green, side1, after, side2, out1, out2):
    del after
    for slot, out in ((0, out1), (1, out2)):
        tile = s_ref[slot]

        def step(n, carry):
            r = pl.multiple_of(n * 16, 16)
            aggregate_rows(
                weights,
                lambda e, l: side1[e, l, tile, pl.ds(r + side1_row, 16)],
                lambda e, l: green[e, l, tile, pl.ds(r + row, 16)],
                lambda e, l: side2[e, l, tile, pl.ds(r, 16)],
                out,
                r,
            )
            return carry

        lax.fori_loop(0, out.shape[2] // 16, step, 0, unroll=4)


TRANSPOSED = (((1,), (1,)), ((), ()))


def right_products(part, weight, p):
    rows = part.shape[2]
    lhs = part[:, :, :, p * 128 : (p + 1) * 128].reshape(16 * rows, 128)
    u = lax.dot_general(lhs, weight, TRANSPOSED, preferred_element_type=jnp.float32)
    return u.astype(BF16).reshape(16, rows, weight.shape[0])


def inner_kernel(s_ref, eff, late1, late2, early1, early2, out, work):
    tau = [s_ref[0], s_ref[1]]
    pair = [
        jnp.concatenate([eff[tau[0], 1], eff[tau[1], 2 - 2 * tau[1]]], axis=0),
        jnp.concatenate([eff[tau[0], 2 - 2 * tau[0]], eff[tau[1], 1]], axis=0),
    ]
    raw = early1.shape[2]
    for source, parts in enumerate(((early1, late1), (early2, late2))):
        for part, row in zip(parts, (0, raw)):
            for p in range(2):
                u = right_products(part, pair[source], p)
                at = pl.ds(source * 128 + row, part.shape[2])
                for a in range(2):
                    work[a, :, at, p * 128 : (p + 1) * 128] = u[:, :, a * 128 : (a + 1) * 128]
    stack = [
        jnp.concatenate([eff[tau[0], 1], eff[tau[0], 2 - 2 * tau[0]]], axis=1),
        jnp.concatenate([eff[tau[1], 2 - 2 * tau[1]], eff[tau[1], 1]], axis=1),
    ]

    def step(e, carry):
        for k in range(4):
            for a in range(2):
                out[e, k, a] = jnp.dot(
                    stack[a], work[a, 4 * e + k], preferred_element_type=jnp.float32
                )
        return carry

    lax.fori_loop(0, 4, step, 0, unroll=2)


def late_kernel(s_ref, eff, late2, late1, out):
    for a, part in enumerate((late1, late2)):
        rim = eff[s_ref[a], 2 * s_ref[a]]
        for p in range(2):
            out[a, :, :, p * 128 : (p + 1) * 128] = right_products(part, rim, p)


def final_kernel(
    s_ref, eff, inner, late, weights, raw1, raw2, far1, far2, out, early1, early2, work, store, sems
):
    tau = [s_ref[0], s_ref[1]]
    rim = [eff[tau[a], 2 * tau[a]] for a in range(2)]
    rows = raw1.shape[2]
    for a, (raw, early) in enumerate(((raw1, early1), (raw2, early2))):

        def step(n, carry):
            r = pl.multiple_of(n * 16, 16)
            aggregate_rows(
                weights,
                lambda e, l: far1[8 * e + 2 * l + a, pl.ds(r, 16)],
                lambda e, l: raw[e, l, pl.ds(r, 16)],
                lambda e, l: far2[8 * e + 2 * l + a, pl.ds(r, 16)],
                early,
                r,
            )
            return carry

        lax.fori_loop(0, rows // 16, step, 0, unroll=4)
        for p in range(2):
            work[a, :, :, p * 128 : (p + 1) * 128] = right_products(early, rim[a], p)

    copies = []
    for e in range(4):
        for k in range(4):
            for a in range(2):
                right = jnp.concatenate([work[a, 4 * e + k], late[a, 4 * e + k]], axis=0)
                total = jnp.dot(rim[a], right, preferred_element_type=jnp.float32)
                store[e, k, tau[a]] = (inner[e, k, a] + total).astype(BF16)
        copies.append(pltpu.make_async_copy(store.at[e], out.at[e], sems.at[e]))
        copies[-1].start()
    for copy in copies:
        copy.wait()


def call(kernel, in_specs, shapes, args, name, out_specs=None, scratch=(), cost=1):
    out_specs = [VMEM] * len(shapes) if out_specs is None else out_specs
    return pl.pallas_call(
        kernel,
        in_specs=in_specs,
        out_specs=out_specs,
        out_shape=[jax.ShapeDtypeStruct(shape, dtype) for shape, dtype in shapes],
        scratch_shapes=list(scratch),
        compiler_params=PARAMS,
        cost_estimate=pl.CostEstimate(flops=cost, bytes_accessed=1, transcendentals=0),
        name=name,
    )(*args)


def local(green, occupation, offsets, qtable, coupling, pattern):
    e_axes = ("em", "rep")
    x1, x2 = swap_pairs(lax.axis_size("blk"), 0), swap_pairs(lax.axis_size("blk"), 1)
    y_count = lax.axis_size(e_axes)
    y1, y2 = swap_pairs(y_count, 0), swap_pairs(y_count, 1)
    odd = lax.axis_index("rep") % 2
    tau1 = 1 - lax.axis_index("blk") % 2
    scalars = jnp.stack([tau1, 1 - tau1, odd]).astype(jnp.int32)
    late = green.shape[3] - RAW
    dma = pltpu.SemaphoreType.DMA
    tile_raw, tile_late = ((4, 4, RAW, 256), BF16), ((4, 4, late, 256), BF16)

    raw2, raw1, late2, whole1, early2 = call(
        load_kernel,
        [SMEM, VMEM],
        [tile_raw, tile_raw]
        + [((2, 4, 2, rows, 256), BF16) for rows in (late, late + RAW, RAW)],
        (scalars, green),
        "load",
    )
    raw2 = lax.ppermute(raw2, "blk", x2)
    raw1 = lax.ppermute(raw1, "blk", x1)
    late2 = lax.ppermute(late2, e_axes, y2)
    whole1 = lax.ppermute(whole1, e_axes, y1)
    early2 = lax.ppermute(early2, e_axes, y2)

    (weights,) = call(
        weight_kernel,
        [SMEM] * 4,
        [((256, 512), BF16)],
        (scalars, occupation, offsets, qtable),
        "weights",
        cost=10**11,
    )
    eff = coupling * pattern[:, :, None, None].astype(BF16)

    def own(row, side1_row, side2, after, shape, name, cost=1):
        def kernel(*refs):
            own_kernel(row, side1_row, *refs)

        return call(
            kernel,
            [SMEM] + [VMEM] * 3 + [ANY, VMEM],
            [shape] * 2,
            (scalars, weights, green, whole1, after, side2),
            name,
            cost=cost,
        )

    own_late1, own_late2 = own(RAW, RAW, late2, whole1, tile_late, "own_late")
    sent2, sent1 = call(
        far_kernel,
        [SMEM, VMEM, VMEM, ANY],
        [((17, RAW, 256), BF16), ((16, RAW, 256), BF16)],
        (scalars, raw2, raw1, own_late1),
        "far",
    )
    rim_late2 = lax.ppermute(own_late2, "blk", x2)
    rim_late1 = lax.ppermute(own_late1, "blk", x1)
    far2 = lax.ppermute(sent2, e_axes, y2)
    far1 = lax.ppermute(sent1, e_axes, y1)
    own_early1, own_early2 = own(0, 0, early2, sent2, tile_raw, "own_early", 1)
    (inner,) = call(
        inner_kernel,
        [SMEM] + [VMEM] * 5,
        [((4, 4, 2, 128, 256), jnp.float32)],
        (scalars, eff, own_late1, own_late2, own_early1, own_early2),
        "inner",
        cost=1,
        scratch=[pltpu.VMEM((2, 16, 256, 256), BF16)],
    )
    (rim_late,) = call(
        late_kernel,
        [SMEM] + [VMEM] * 3,
        [((2, 16, late, 256), BF16)],
        (scalars, eff, rim_late2, rim_late1),
        "late",
        cost=1000000000,
    )
    (sigma,) = call(
        final_kernel,
        [SMEM] + [VMEM] * 8,
        [(green.shape, BF16)],
        (scalars, eff, inner, rim_late, weights, raw1, raw2, far1, far2),
        "final",
        out_specs=[ANY],
        scratch=[
            pltpu.VMEM((4, 4, RAW, 256), BF16),
            pltpu.VMEM((4, 4, RAW, 256), BF16),
            pltpu.VMEM((2, 16, RAW, 256), BF16),
            pltpu.VMEM(green.shape, BF16),
            dma((4,)),
        ],
    )
    return sigma


def solution(mesh):
    in_specs = (
        P(("em", "rep"), None, "blk", None, None),
        P(),
        P(),
        P(),
        P("blk", None, None, None),
        P("blk", None),
    )
    out_specs = P(("em", "rep"), None, "blk", None, None)
    return jax.shard_map(local, mesh=mesh, in_specs=in_specs, out_specs=out_specs, check_vma=False)
```

```python
import jax
import jax.numpy as jnp
from jax import lax
from jax.experimental import pallas as pl
from jax.experimental.pallas import tpu as pltpu
from jax.sharding import PartitionSpec as P

REACH = 2
RAW = 64
VMEM = pl.BlockSpec(memory_space=pltpu.VMEM)
SMEM = pl.BlockSpec(memory_space=pltpu.SMEM)
HBM = pl.BlockSpec(memory_space=pltpu.HBM)
ANY = pl.BlockSpec(memory_space=pl.ANY)
PARAMS = pltpu.CompilerParams(vmem_limit_bytes=40 * 2**20)
BF16 = jnp.bfloat16


def swap_pairs(count, first):
    pairs = [(i, i + 1) for i in range(first, count - 1, 2)]
    return pairs + [(b, a) for a, b in pairs]


def load_kernel(s_ref, green, raw2, raw1, late2, whole1, early2):
    raw = early2.shape[3]
    one, two = 2 - 2 * s_ref[2], 2 * s_ref[2]
    for e in range(4):
        raw2[e] = green[e, :, s_ref[1], :raw]
        raw1[e] = green[e, :, s_ref[0], :raw]
    for e in range(REACH):
        late2[e] = green[two + e, :, :, raw:]
        whole1[e] = green[one + e]
        early2[e] = green[two + e, :, :, :raw]


def far_kernel(s_ref, raw2, raw1, after, far2, far1):
    del after
    one, two = 2 - 2 * s_ref[2], 2 * s_ref[2]
    for slot, raw in enumerate((raw1, raw2)):
        for e in range(REACH):
            for l in range(4):
                far2[8 * e + 2 * l + slot] = raw[two + e, l]
                far1[8 * e + 2 * l + slot] = raw[one + e, l]
    far2[16] = jnp.zeros(far2.shape[1:], BF16)


def weight_kernel(s_ref, occupation, offsets, qtable, early, out, early_out):
    early_out[...] = early[...]

    def band(d):
        total = 0.0
        for s in range(4):
            value = occupation[s] + 1.0 if d > 0 else occupation[s]
            total = total + jnp.where(offsets[s] == abs(d), value, 0.0)
        return total

    bands = {d: band(d) for d in (-2, -1, 1, 2)}
    lane = lax.broadcasted_iota(jnp.int32, (16, 128), 1)
    unit = lax.broadcasted_iota(jnp.int32, (16, 128), 0) == lane % 16
    transfer = []
    for k in range(4):
        row = jnp.zeros((16, 128), jnp.float32)
        for l in range(4):
            hits = sum(jnp.where(qtable[k, q] == l, 0.25, 0.0) for q in range(4))
            row = jnp.where(unit & ((lane // 16) % 4 == l), hits, row)
        transfer.append(row)

    def weight(even, odd):
        low, high = bands.get(even, 0.0), bands.get(odd, 0.0)
        return jnp.where(s_ref[2] == 1, high, low)

    for place, (even, odd) in enumerate(((4, -2), (0, 0), (2, 2), (-2, 4))):
        for e in range(4):
            left = weight(even - e, odd - e)
            right = weight(even - e + 1, odd - e + 1)
            scale = jnp.where(lane < 64, left, right)
            for k in range(4):
                at = pl.ds(64 * e + 16 * k, 16)
                out[at, place * 128 : (place + 1) * 128] = (scale * transfer[k]).astype(BF16)


def aggregate_rows(weights, side1, own, side2, out, out_row):
    blocks = [side1(e, l) for e in range(2) for l in range(4)]
    blocks += [own(e, l) for e in range(4) for l in range(4)]
    blocks += [side2(e, l) for e in range(2) for l in range(4)]
    total = jnp.dot(
        weights[...], jnp.concatenate(blocks, axis=0), preferred_element_type=jnp.float32
    ).astype(BF16)
    for e in range(4):
        for k in range(4):
            n = 16 * (4 * e + k)
            out[e, k, pl.ds(out_row, 16)] = total[n : n + 16]


def own_kernel(row, side1_row, s_ref, weights, green, side1, after, side2, out1, out2):
    del after
    for slot, out in ((0, out1), (1, out2)):
        tile = s_ref[slot]

        def step(n, carry):
            r = pl.multiple_of(n * 16, 16)
            aggregate_rows(
                weights,
                lambda e, l: side1[e, l, tile, pl.ds(r + side1_row, 16)],
                lambda e, l: green[e, l, tile, pl.ds(r + row, 16)],
                lambda e, l: side2[e, l, tile, pl.ds(r, 16)],
                out,
                r,
            )
            return carry

        lax.fori_loop(0, out.shape[2] // 16, step, 0, unroll=4)


TRANSPOSED = (((1,), (1,)), ((), ()))


def right_products(part, weight, p):
    rows = part.shape[2]
    lhs = part[:, :, :, p * 128 : (p + 1) * 128].reshape(16 * rows, 128)
    u = lax.dot_general(lhs, weight, TRANSPOSED, preferred_element_type=jnp.float32)
    return u.astype(BF16).reshape(16, rows, weight.shape[0])


def inner_kernel(s_ref, eff, late1, late2, early1, early2, out, work):
    tau = [s_ref[0], s_ref[1]]
    pair = [
        jnp.concatenate([eff[tau[0], 1], eff[tau[1], 2 - 2 * tau[1]]], axis=0),
        jnp.concatenate([eff[tau[0], 2 - 2 * tau[0]], eff[tau[1], 1]], axis=0),
    ]
    raw = early1.shape[2]
    for source, parts in enumerate(((early1, late1), (early2, late2))):
        for part, row in zip(parts, (0, raw)):
            for p in range(2):
                u = right_products(part, pair[source], p)
                at = pl.ds(source * 128 + row, part.shape[2])
                for a in range(2):
                    work[a, :, at, p * 128 : (p + 1) * 128] = u[:, :, a * 128 : (a + 1) * 128]
    stack = [
        jnp.concatenate([eff[tau[0], 1], eff[tau[0], 2 - 2 * tau[0]]], axis=1),
        jnp.concatenate([eff[tau[1], 2 - 2 * tau[1]], eff[tau[1], 1]], axis=1),
    ]

    def step(e, carry):
        for k in range(4):
            for a in range(2):
                out[e, k, a] = jnp.dot(
                    stack[a], work[a, 4 * e + k], preferred_element_type=jnp.float32
                )
        return carry

    lax.fori_loop(0, 4, step, 0, unroll=2)


def late_kernel(s_ref, eff, late2, late1, out):
    for a, part in enumerate((late1, late2)):
        rim = eff[s_ref[a], 2 * s_ref[a]]
        for p in range(2):
            out[a, :, :, p * 128 : (p + 1) * 128] = right_products(part, rim, p)


def final_kernel(
    s_ref, eff, inner, late, weights, raw1, raw2, far1, far2, out, early1, early2, work, store, sems
):
    tau = [s_ref[0], s_ref[1]]
    rim = [eff[tau[a], 2 * tau[a]] for a in range(2)]
    rows = raw1.shape[2]
    for a, (raw, early) in enumerate(((raw1, early1), (raw2, early2))):

        def step(n, carry):
            r = pl.multiple_of(n * 16, 16)
            aggregate_rows(
                weights,
                lambda e, l: far1[8 * e + 2 * l + a, pl.ds(r, 16)],
                lambda e, l: raw[e, l, pl.ds(r, 16)],
                lambda e, l: far2[8 * e + 2 * l + a, pl.ds(r, 16)],
                early,
                r,
            )
            return carry

        lax.fori_loop(0, rows // 16, step, 0, unroll=4)
        for p in range(2):
            work[a, :, :, p * 128 : (p + 1) * 128] = right_products(early, rim[a], p)

    copies = []
    for e in range(4):
        for k in range(4):
            for a in range(2):
                right = jnp.concatenate([work[a, 4 * e + k], late[a, 4 * e + k]], axis=0)
                total = jnp.dot(rim[a], right, preferred_element_type=jnp.float32)
                store[e, k, tau[a]] = (inner[e, k, a] + total).astype(BF16)
        copies.append(pltpu.make_async_copy(store.at[e], out.at[e], sems.at[e]))
        copies[-1].start()
    for copy in copies:
        copy.wait()


def call(kernel, in_specs, shapes, args, name, out_specs=None, scratch=(), cost=1):
    out_specs = [VMEM] * len(shapes) if out_specs is None else out_specs
    return pl.pallas_call(
        kernel,
        in_specs=in_specs,
        out_specs=out_specs,
        out_shape=[jax.ShapeDtypeStruct(shape, dtype) for shape, dtype in shapes],
        scratch_shapes=list(scratch),
        compiler_params=PARAMS,
        cost_estimate=pl.CostEstimate(flops=cost, bytes_accessed=1, transcendentals=0),
        name=name,
    )(*args)


def local(green, occupation, offsets, qtable, coupling, pattern):
    e_axes = ("em", "rep")
    x1, x2 = swap_pairs(lax.axis_size("blk"), 0), swap_pairs(lax.axis_size("blk"), 1)
    y_count = lax.axis_size(e_axes)
    y1, y2 = swap_pairs(y_count, 0), swap_pairs(y_count, 1)
    odd = lax.axis_index("rep") % 2
    tau1 = 1 - lax.axis_index("blk") % 2
    scalars = jnp.stack([tau1, 1 - tau1, odd]).astype(jnp.int32)
    late = green.shape[3] - RAW
    dma = pltpu.SemaphoreType.DMA
    tile_raw, tile_late = ((4, 4, RAW, 256), BF16), ((4, 4, late, 256), BF16)

    raw2, raw1, late2, whole1, early2 = call(
        load_kernel,
        [SMEM, VMEM],
        [tile_raw, tile_raw]
        + [((2, 4, 2, rows, 256), BF16) for rows in (late, late + RAW, RAW)],
        (scalars, green),
        "load",
    )
    raw2 = lax.ppermute(raw2, "blk", x2)
    raw1 = lax.ppermute(raw1, "blk", x1)
    late2 = lax.ppermute(late2, e_axes, y2)
    whole1 = lax.ppermute(whole1, e_axes, y1)

    weights, early2 = call(
        weight_kernel,
        [SMEM] * 4 + [VMEM],
        [((256, 512), BF16), (early2.shape, BF16)],
        (scalars, occupation, offsets, qtable, early2),
        "weights",
        cost=10**11,
    )
    early2 = lax.ppermute(early2, e_axes, y2)
    eff = coupling * pattern[:, :, None, None].astype(BF16)

    def own(row, side1_row, side2, after, shape, name, cost=1):
        def kernel(*refs):
            own_kernel(row, side1_row, *refs)

        return call(
            kernel,
            [SMEM] + [VMEM] * 3 + [ANY, VMEM],
            [shape] * 2,
            (scalars, weights, green, whole1, after, side2),
            name,
            cost=cost,
        )

    own_late1, own_late2 = own(RAW, RAW, late2, whole1, tile_late, "own_late")
    sent2, sent1 = call(
        far_kernel,
        [SMEM, VMEM, VMEM, ANY],
        [((17, RAW, 256), BF16), ((16, RAW, 256), BF16)],
        (scalars, raw2, raw1, own_late1),
        "far",
    )
    rim_late2 = lax.ppermute(own_late2, "blk", x2)
    rim_late1 = lax.ppermute(own_late1, "blk", x1)
    far2 = lax.ppermute(sent2, e_axes, y2)
    far1 = lax.ppermute(sent1, e_axes, y1)
    own_early1, own_early2 = own(0, 0, early2, sent2, tile_raw, "own_early", 1)
    (inner,) = call(
        inner_kernel,
        [SMEM] + [VMEM] * 5,
        [((4, 4, 2, 128, 256), jnp.float32)],
        (scalars, eff, own_late1, own_late2, own_early1, own_early2),
        "inner",
        cost=1,
        scratch=[pltpu.VMEM((2, 16, 256, 256), BF16)],
    )
    (rim_late,) = call(
        late_kernel,
        [SMEM] + [VMEM] * 3,
        [((2, 16, late, 256), BF16)],
        (scalars, eff, rim_late2, rim_late1),
        "late",
        cost=1000000000,
    )
    (sigma,) = call(
        final_kernel,
        [SMEM] + [VMEM] * 8,
        [(green.shape, BF16)],
        (scalars, eff, inner, rim_late, weights, raw1, raw2, far1, far2),
        "final",
        out_specs=[ANY],
        scratch=[
            pltpu.VMEM((4, 4, RAW, 256), BF16),
            pltpu.VMEM((4, 4, RAW, 256), BF16),
            pltpu.VMEM((2, 16, RAW, 256), BF16),
            pltpu.VMEM(green.shape, BF16),
            dma((4,)),
        ],
    )
    return sigma


def solution(mesh):
    in_specs = (
        P(("em", "rep"), None, "blk", None, None),
        P(),
        P(),
        P(),
        P("blk", None, None, None),
        P("blk", None),
    )
    out_specs = P(("em", "rep"), None, "blk", None, None)
    return jax.shard_map(local, mesh=mesh, in_specs=in_specs, out_specs=out_specs, check_vma=False)
```

```python
import jax
import jax.numpy as jnp
from jax import lax
from jax.experimental import pallas as pl
from jax.experimental.pallas import tpu as pltpu
from jax.sharding import PartitionSpec as P

REACH = 2
RAW = 64
VMEM = pl.BlockSpec(memory_space=pltpu.VMEM)
SMEM = pl.BlockSpec(memory_space=pltpu.SMEM)
HBM = pl.BlockSpec(memory_space=pltpu.HBM)
ANY = pl.BlockSpec(memory_space=pl.ANY)
PARAMS = pltpu.CompilerParams(vmem_limit_bytes=40 * 2**20)
BF16 = jnp.bfloat16


def swap_pairs(count, first):
    pairs = [(i, i + 1) for i in range(first, count - 1, 2)]
    return pairs + [(b, a) for a, b in pairs]


def load_kernel(s_ref, green, raw2, raw1, late2, whole1, early2):
    raw = early2.shape[3]
    one, two = 2 - 2 * s_ref[2], 2 * s_ref[2]
    for e in range(4):
        raw2[e] = green[e, :, s_ref[1], :raw]
        raw1[e] = green[e, :, s_ref[0], :raw]
    for e in range(REACH):
        late2[e] = green[two + e, :, :, raw:]
        whole1[e] = green[one + e]
        early2[e] = green[two + e, :, :, :raw]


def far_kernel(s_ref, raw2, raw1, after, far2, far1):
    del after
    one, two = 2 - 2 * s_ref[2], 2 * s_ref[2]
    for slot, raw in enumerate((raw1, raw2)):
        for e in range(REACH):
            for l in range(4):
                far2[8 * e + 2 * l + slot] = raw[two + e, l]
                far1[8 * e + 2 * l + slot] = raw[one + e, l]


def weight_kernel(s_ref, occupation, offsets, qtable, early, out, early_out):
    early_out[...] = early[...]

    def band(d):
        total = 0.0
        for s in range(4):
            value = occupation[s] + 1.0 if d > 0 else occupation[s]
            total = total + jnp.where(offsets[s] == abs(d), value, 0.0)
        return total

    bands = {d: band(d) for d in (-2, -1, 1, 2)}
    lane = lax.broadcasted_iota(jnp.int32, (16, 128), 1)
    unit = lax.broadcasted_iota(jnp.int32, (16, 128), 0) == lane % 16
    transfer = []
    for k in range(4):
        row = jnp.zeros((16, 128), jnp.float32)
        for l in range(4):
            hits = sum(jnp.where(qtable[k, q] == l, 0.25, 0.0) for q in range(4))
            row = jnp.where(unit & ((lane // 16) % 4 == l), hits, row)
        transfer.append(row)

    def weight(even, odd):
        low, high = bands.get(even, 0.0), bands.get(odd, 0.0)
        return jnp.where(s_ref[2] == 1, high, low)

    for place, (even, odd) in enumerate(((4, -2), (0, 0), (2, 2), (-2, 4))):
        for e in range(4):
            left = weight(even - e, odd - e)
            right = weight(even - e + 1, odd - e + 1)
            scale = jnp.where(lane < 64, left, right)
            for k in range(4):
                at = pl.ds(64 * e + 16 * k, 16)
                out[at, place * 128 : (place + 1) * 128] = (scale * transfer[k]).astype(BF16)


def aggregate_rows(weights, side1, own, side2, out, out_row):
    blocks = [side1(e, l) for e in range(2) for l in range(4)]
    blocks += [own(e, l) for e in range(4) for l in range(4)]
    blocks += [side2(e, l) for e in range(2) for l in range(4)]
    total = jnp.dot(
        weights[...], jnp.concatenate(blocks, axis=0), preferred_element_type=jnp.float32
    ).astype(BF16)
    for e in range(4):
        for k in range(4):
            n = 16 * (4 * e + k)
            out[e, k, pl.ds(out_row, 16)] = total[n : n + 16]


def own_kernel(row, side1_row, s_ref, weights, green, side1, after, side2, out1, out2):
    del after
    for slot, out in ((0, out1), (1, out2)):
        tile = s_ref[slot]

        def step(n, carry):
            r = pl.multiple_of(n * 16, 16)
            aggregate_rows(
                weights,
                lambda e, l: side1[e, l, tile, pl.ds(r + side1_row, 16)],
                lambda e, l: green[e, l, tile, pl.ds(r + row, 16)],
                lambda e, l: side2[e, l, tile, pl.ds(r, 16)],
                out,
                r,
            )
            return carry

        lax.fori_loop(0, out.shape[2] // 16, step, 0, unroll=4)


TRANSPOSED = (((1,), (1,)), ((), ()))


def right_products(part, weight, p):
    rows = part.shape[2]
    lhs = part[:, :, :, p * 128 : (p + 1) * 128].reshape(16 * rows, 128)
    u = lax.dot_general(lhs, weight, TRANSPOSED, preferred_element_type=jnp.float32)
    return u.astype(BF16).reshape(16, rows, weight.shape[0])


def inner_kernel(s_ref, eff, late1, late2, early1, early2, out, work):
    tau = [s_ref[0], s_ref[1]]
    pair = [
        jnp.concatenate([eff[tau[0], 1], eff[tau[1], 2 - 2 * tau[1]]], axis=0),
        jnp.concatenate([eff[tau[0], 2 - 2 * tau[0]], eff[tau[1], 1]], axis=0),
    ]
    raw = early1.shape[2]
    for source, parts in enumerate(((early1, late1), (early2, late2))):
        for part, row in zip(parts, (0, raw)):
            for p in range(2):
                u = right_products(part, pair[source], p)
                at = pl.ds(source * 128 + row, part.shape[2])
                for a in range(2):
                    work[a, :, at, p * 128 : (p + 1) * 128] = u[:, :, a * 128 : (a + 1) * 128]
    stack = [
        jnp.concatenate([eff[tau[0], 1], eff[tau[0], 2 - 2 * tau[0]]], axis=1),
        jnp.concatenate([eff[tau[1], 2 - 2 * tau[1]], eff[tau[1], 1]], axis=1),
    ]

    def step(e, carry):
        for k in range(4):
            for a in range(2):
                out[e, k, a] = jnp.dot(
                    stack[a], work[a, 4 * e + k], preferred_element_type=jnp.float32
                )
        return carry

    lax.fori_loop(0, 4, step, 0, unroll=2)


def late_kernel(s_ref, eff, late2, late1, out):
    for a, part in enumerate((late1, late2)):
        rim = eff[s_ref[a], 2 * s_ref[a]]
        for p in range(2):
            out[a, :, :, p * 128 : (p + 1) * 128] = right_products(part, rim, p)


def final_kernel(
    s_ref, eff, inner, late, weights, raw1, raw2, far1, far2, out, early1, early2, work, store, sems
):
    tau = [s_ref[0], s_ref[1]]
    rim = [eff[tau[a], 2 * tau[a]] for a in range(2)]
    rows = raw1.shape[2]
    for a, (raw, early) in enumerate(((raw1, early1), (raw2, early2))):

        def step(n, carry):
            r = pl.multiple_of(n * 16, 16)
            aggregate_rows(
                weights,
                lambda e, l: far1[8 * e + 2 * l + a, pl.ds(r, 16)],
                lambda e, l: raw[e, l, pl.ds(r, 16)],
                lambda e, l: far2[8 * e + 2 * l + a, pl.ds(r, 16)],
                early,
                r,
            )
            return carry

        lax.fori_loop(0, rows // 16, step, 0, unroll=4)
        for p in range(2):
            work[a, :, :, p * 128 : (p + 1) * 128] = right_products(early, rim[a], p)

    copies = []
    for e in range(4):
        for k in range(4):
            for a in range(2):
                right = jnp.concatenate([work[a, 4 * e + k], late[a, 4 * e + k]], axis=0)
                total = jnp.dot(rim[a], right, preferred_element_type=jnp.float32)
                store[e, k, tau[a]] = (inner[e, k, a] + total).astype(BF16)
        copies.append(pltpu.make_async_copy(store.at[e], out.at[e], sems.at[e]))
        copies[-1].start()
    for copy in copies:
        copy.wait()


def call(kernel, in_specs, shapes, args, name, out_specs=None, scratch=(), cost=1):
    out_specs = [VMEM] * len(shapes) if out_specs is None else out_specs
    return pl.pallas_call(
        kernel,
        in_specs=in_specs,
        out_specs=out_specs,
        out_shape=[jax.ShapeDtypeStruct(shape, dtype) for shape, dtype in shapes],
        scratch_shapes=list(scratch),
        compiler_params=PARAMS,
        cost_estimate=pl.CostEstimate(flops=cost, bytes_accessed=1, transcendentals=0),
        name=name,
    )(*args)


def local(green, occupation, offsets, qtable, coupling, pattern):
    e_axes = ("em", "rep")
    x1, x2 = swap_pairs(lax.axis_size("blk"), 0), swap_pairs(lax.axis_size("blk"), 1)
    y_count = lax.axis_size(e_axes)
    y1, y2 = swap_pairs(y_count, 0), swap_pairs(y_count, 1)
    odd = lax.axis_index("rep") % 2
    tau1 = 1 - lax.axis_index("blk") % 2
    scalars = jnp.stack([tau1, 1 - tau1, odd]).astype(jnp.int32)
    late = green.shape[3] - RAW
    dma = pltpu.SemaphoreType.DMA
    tile_raw, tile_late = ((4, 4, RAW, 256), BF16), ((4, 4, late, 256), BF16)

    raw2, raw1, late2, whole1, early2 = call(
        load_kernel,
        [SMEM, VMEM],
        [tile_raw, tile_raw]
        + [((2, 4, 2, rows, 256), BF16) for rows in (late, late + RAW, RAW)],
        (scalars, green),
        "load",
    )
    raw2 = lax.ppermute(raw2, "blk", x2)
    raw1 = lax.ppermute(raw1, "blk", x1)
    late2 = lax.ppermute(late2, e_axes, y2)
    whole1 = lax.ppermute(whole1, e_axes, y1)

    weights, early2 = call(
        weight_kernel,
        [SMEM] * 4 + [VMEM],
        [((256, 512), BF16), (early2.shape, BF16)],
        (scalars, occupation, offsets, qtable, early2),
        "weights",
        cost=10**11,
    )
    early2 = lax.ppermute(early2, e_axes, y2)
    eff = coupling * pattern[:, :, None, None].astype(BF16)

    def own(row, side1_row, side2, after, shape, name, cost=1):
        def kernel(*refs):
            own_kernel(row, side1_row, *refs)

        return call(
            kernel,
            [SMEM] + [VMEM] * 3 + [ANY, VMEM],
            [shape] * 2,
            (scalars, weights, green, whole1, after, side2),
            name,
            cost=cost,
        )

    own_late1, own_late2 = own(RAW, RAW, late2, whole1, tile_late, "own_late")
    sent2, sent1 = call(
        far_kernel,
        [SMEM, VMEM, VMEM, ANY],
        [((16, RAW, 256), BF16)] * 2,
        (scalars, raw2, raw1, own_late1),
        "far",
    )
    rim_late2 = lax.ppermute(own_late2, "blk", x2)
    rim_late1 = lax.ppermute(own_late1, "blk", x1)
    far2 = lax.ppermute(sent2.reshape(2, 8, RAW, 256), e_axes, y2).reshape(16, RAW, 256)
    far1 = lax.ppermute(sent1, e_axes, y1)
    own_early1, own_early2 = own(0, 0, early2, sent2, tile_raw, "own_early", 1)
    (inner,) = call(
        inner_kernel,
        [SMEM] + [VMEM] * 5,
        [((4, 4, 2, 128, 256), jnp.float32)],
        (scalars, eff, own_late1, own_late2, own_early1, own_early2),
        "inner",
        cost=1,
        scratch=[pltpu.VMEM((2, 16, 256, 256), BF16)],
    )
    (rim_late,) = call(
        late_kernel,
        [SMEM] + [VMEM] * 3,
        [((2, 16, late, 256), BF16)],
        (scalars, eff, rim_late2, rim_late1),
        "late",
        cost=1000000000,
    )
    (sigma,) = call(
        final_kernel,
        [SMEM] + [VMEM] * 8,
        [(green.shape, BF16)],
        (scalars, eff, inner, rim_late, weights, raw1, raw2, far1, far2),
        "final",
        out_specs=[ANY],
        scratch=[
            pltpu.VMEM((4, 4, RAW, 256), BF16),
            pltpu.VMEM((4, 4, RAW, 256), BF16),
            pltpu.VMEM((2, 16, RAW, 256), BF16),
            pltpu.VMEM(green.shape, BF16),
            dma((4,)),
        ],
    )
    return sigma


def solution(mesh):
    in_specs = (
        P(("em", "rep"), None, "blk", None, None),
        P(),
        P(),
        P(),
        P("blk", None, None, None),
        P("blk", None),
    )
    out_specs = P(("em", "rep"), None, "blk", None, None)
    return jax.shard_map(local, mesh=mesh, in_specs=in_specs, out_specs=out_specs, check_vma=False)
```
